32 devices in a mesh: ep: 8 (over z, x), node: 2 (over core), dp: 2 (over y).
Axes of the slice: x: 2, y: 2, z: 4, core: 2. Of those that a mesh axis runs over, the one named last changes fastest.
Arguments:
- grad_out: bfloat16 [2048, 7168], P(('ep', 'node'), 'dp'), may hold values from -6 to 6
- tokens: bfloat16 [2048, 7168], P(('ep', 'node'), 'dp'), may hold values from -0.59765625 to 0.59765625
- scores: float32 [2048, 16], P(('ep', 'node')), may hold values from 0.02 to 0.98
- expert_ids: int32 [2048, 8], P(('ep', 'node')), may hold values from 0 to 15, all different within a row; in each aligned block of 128 rows (0 to 127, 128 to 255, ...) at most 80 rows name the same one
- hidden_act: bfloat16 [16, 1280, 1024], P(('ep', 'node')), may hold values from -0.29882812 to 0.29882812
- down_weight: bfloat16 [16, 1024, 7168], P(('ep', 'node'), None, 'dp'), may hold values from -0.1875 to 0.1875
Outputs:
- weight_grad: bfloat16 [16, 1024, 7168], P(('ep', 'node'), None, 'dp')
- hidden_grad: bfloat16 [16, 1280, 1024], P(('ep', 'node'), 'dp')
- gate_grad: float32 [16, 7168], P(None, 'dp')
The draws below stay inside these ranges and needn't reach their ends.
Inputs may be any that keep to these rules, and one draw needn't show every extreme that they name: `expert_ids`: among the routes of the 128 tokens of one source device, no expert is named more than 80 times, a bound that some block reaches.
All inputs are finite; a program needn't handle non-finite values.
Results may differ from the reference program's by a relative error of at most 0.017.
Values may be sent and summed in bfloat16 or wider, within the bound.
A program may use at most 128 MiB of HBM per device.

```python
import math
import jax
import jax.numpy as jnp
import numpy as np
from jax import lax

D = 7168
F = 1024
TOPK = 8
TOK_DEV = 128
EXPERTS = 16
MOST = 80
SLOTS = 1280
TOKENS = 2048
N_DP = 2


def levels(rng, extent, split, low, largest):
    def one(position, blocks):
        steps = jax.random.uniform(jax.random.fold_in(jax.random.fold_in(rng, 6), position), (blocks,), jnp.float32, low / len(split), largest / len(split))
        return jnp.repeat(jnp.exp(steps), extent[position] // blocks).reshape((-1,) + (1,) * (len(extent) - position - 1))

    gain = one(*split[0])
    for cut in split[1:]:
        gain = gain * one(*cut)
    return gain


def deal_out(own_key, own, number, rows, number_of, top, limit, slope):
    sequence = jax.random.permutation(own_key, number_of)
    packed, common = portions_of(number_of, rows * top, limit, slope, True), portions_of(number_of, rows * top, limit, slope, False)
    places = jnp.arange(number_of)

    def named(sizes, offset_by):
        used = int((sizes > 0).sum())
        fixed = max(1, used // 4)
        passed = fixed + (places - fixed + offset_by * (used - fixed)) % max(1, number_of - fixed)
        return jnp.zeros((number_of,), jnp.int32).at[sequence[jnp.where(places < fixed, places, passed)]].set(jnp.asarray(sizes, jnp.int32))

    sizes = jnp.where(number % 4 == 0, named(packed, number // 4), named(common, number - number // 4 - 1))
    mixed = jax.random.permutation(jax.random.fold_in(own, 3), number_of)
    donor, taker = mixed[0:number_of // 2 * 2:2], mixed[1:number_of // 2 * 2:2]
    room = jnp.minimum(sizes[donor] - 1, limit - sizes[taker]) // 2
    room = jnp.where((donor == sequence[0]) | (taker == sequence[0]) | (sizes[taker] == 0), 0, jnp.maximum(room, 0))
    passed = jax.random.randint(jax.random.fold_in(own, 4), (number_of // 2,), 0, 1 << 20) % (room + 1)
    sizes = sizes.at[donor].add(-passed).at[taker].add(passed)
    labels = jnp.searchsorted(jnp.cumsum(sizes), jnp.arange(rows * top), side="right").astype(jnp.int32)
    listing = labels.reshape(top, rows).T
    listing = listing[jax.random.permutation(jax.random.fold_in(own, 1), rows)]
    offset_by = jax.random.randint(jax.random.fold_in(own, 2), (rows, 1), 0, top)
    return jnp.take_along_axis(listing, (jnp.arange(top)[None, :] + offset_by) % top, axis=1)


def portions_of(count, total, bound, slope, full):
    portions = [(1 << 20) // math.isqrt(rank ** slope) + 1 for rank in range(1, count + 1)]
    largest = bound if full else min(bound, max(-(-total // count), total * portions[0] // sum(portions)))
    least = 1 if total - largest >= count - 1 else 0
    counts, rest = [largest] + [least] * (count - 1), total - largest - least * (count - 1)
    while rest > 0:
        movable = [i for i in range(1, count) if counts[i] < largest] or [i for i in range(1, count) if counts[i] < bound]
        whole, remaining = sum([portions[i] for i in movable]), rest
        for i in movable:
            extra = min(bound - counts[i], max(1, remaining * portions[i] // whole), rest)
            counts[i] = counts[i] + extra
            rest = rest - extra
    return np.array(counts)


def centred(own_key, dims, scale, limit, split=(), held_as=jnp.bfloat16):
    loudness = levels(own_key, dims, split, -0.22, 0.18) if split else 1.0
    array = jax.random.normal(own_key, dims, jnp.float32) * scale * loudness
    return jnp.minimum(jnp.maximum(array, -limit), limit).astype(held_as)


def setup_inputs(seed: int = 0) -> dict:
    arg_keys = jax.random.split(jax.random.key(seed), 7)
    grad_out = centred(arg_keys[0], (TOKENS, D), 1.0, 6.0, ((0, 16), (1, 2)))
    tokens = centred(arg_keys[1], (TOKENS, D), 0.1, 0.59765625, ((0, 16), (1, 2)))
    scores = jnp.clip(0.02 + 0.96000002 * jax.random.uniform(arg_keys[2], (TOKENS, EXPERTS), jnp.float32) ** levels(arg_keys[2], (TOKENS, EXPERTS), ((0, 16),), -0.2, 0.2), 0.02, 0.98)
    expert_ids_keys = jax.random.split(jax.random.fold_in(arg_keys[3], 1), TOKENS // TOK_DEV)
    expert_ids_turns = jax.random.permutation(jax.random.fold_in(arg_keys[3], 3), TOKENS // TOK_DEV)
    expert_ids = jax.vmap(lambda own, number: deal_out(jax.random.fold_in(arg_keys[3], 2), own, number, TOK_DEV, EXPERTS, TOPK, MOST, 2))(expert_ids_keys, expert_ids_turns).reshape((TOKENS, TOPK))
    hidden_act = centred(arg_keys[4], (EXPERTS, SLOTS, F), 0.05, 0.29882812, ((0, 16),))
    down_weight = centred(arg_keys[5], (EXPERTS, F, D), F ** -0.5, 0.1875, ((0, 16), (2, 2)))
    return dict(grad_out=grad_out, tokens=tokens, scores=scores, expert_ids=expert_ids, hidden_act=hidden_act, down_weight=down_weight)


route_scale = 2.5


def reference(grad_out, tokens, scores, expert_ids, hidden_act, down_weight):
    chosen = jnp.take_along_axis(scores, expert_ids, axis=1)
    total = jnp.sum(chosen, axis=1, keepdims=True)
    weights = (route_scale * chosen / total).astype(jnp.bfloat16)
    flat_ids = expert_ids.reshape(EXPERTS, TOK_DEV * TOPK)
    onehot = (flat_ids[:, :, None] == jnp.arange(EXPERTS, dtype=jnp.int32)[None, None, :]).astype(jnp.int32)
    before = jnp.cumsum(onehot, axis=1) - onehot
    rank = jnp.sum(before * onehot, axis=2)
    source = jnp.arange(EXPERTS, dtype=jnp.int32)[:, None]
    target = (flat_ids * SLOTS + source * MOST + rank).reshape(TOKENS * TOPK).astype(jnp.int32)
    route_index = jnp.arange(TOKENS * TOPK, dtype=jnp.int32)
    owner = jnp.full((EXPERTS * SLOTS,), -1, jnp.int32).at[target].set(route_index)
    owner = owner.reshape(EXPERTS, SLOTS)
    flat_weights = weights.reshape(TOKENS * TOPK)
    block_cols = D // N_DP

    def per_expert(operands):
        rows_of, hidden, down = operands
        valid = rows_of >= 0
        safe_rows = jnp.where(valid, rows_of, 0).astype(jnp.int32)
        rows = jnp.where(valid[:, None], grad_out[safe_rows // TOPK], jnp.zeros((), grad_out.dtype))
        gains = jnp.where(valid, flat_weights[safe_rows], jnp.zeros((), flat_weights.dtype))
        scaled = (gains.astype(jnp.float32)[:, None] * rows.astype(jnp.float32)).astype(jnp.bfloat16)
        weight_grad = lax.dot_general(hidden, scaled, (((0,), (0,)), ((), ())), preferred_element_type=jnp.float32).astype(jnp.bfloat16)
        outputs = jnp.dot(hidden, down, preferred_element_type=jnp.float32)
        slot_grad = jnp.sum(outputs * rows.astype(jnp.float32), axis=1)
        scaled_blocks = scaled.astype(jnp.float32).reshape(SLOTS, N_DP, block_cols)
        down_blocks = down.astype(jnp.float32).reshape(F, N_DP, block_cols)
        partials = jnp.einsum("snd,fnd->nsf", scaled_blocks, down_blocks, precision=lax.Precision.HIGHEST)
        rounded = lax.optimization_barrier(partials.astype(jnp.bfloat16))
        hidden_grad = jnp.sum(rounded.astype(jnp.float32), axis=0).astype(jnp.bfloat16)
        return weight_grad, hidden_grad, slot_grad

    weight_grad, hidden_grad, slot_grad = lax.map(per_expert, (owner, hidden_act, down_weight))
    route_grad = slot_grad.reshape(EXPERTS * SLOTS)[target].reshape(TOKENS, TOPK)
    mixed = jnp.sum(route_grad * chosen, axis=1, keepdims=True) / total
    score_grad = route_scale / total * (route_grad - mixed)
    logit_sel = score_grad * chosen * (1.0 - chosen)
    onehot_k = (expert_ids[:, :, None] == jnp.arange(EXPERTS, dtype=jnp.int32)[None, None, :]).astype(jnp.float32)
    logit_grad = jnp.sum(logit_sel[:, :, None] * onehot_k, axis=1).astype(jnp.bfloat16)
    gate_grad = jnp.dot(logit_grad.T, tokens, preferred_element_type=jnp.float32)
    return weight_grad, hidden_grad, gate_grad
```

```python
import jax
import jax.numpy as jnp
from jax import lax
from jax.sharding import PartitionSpec as P

route_scale = 2.5
AX = ("ep", "node")
f32, bf16 = jnp.float32, jnp.bfloat16


def router(scores, expert_ids):
    tok = expert_ids.shape[0]
    experts = scores.shape[1]
    ids_t = expert_ids.T
    names = lax.broadcasted_iota(jnp.int32, (experts, tok), 0)
    mask = jnp.zeros((experts, tok), f32)
    for k in range(expert_ids.shape[1]):
        mask = mask + (ids_t[k][None, :] == names).astype(f32)
    chosen = mask * scores.T
    total = jnp.sum(chosen, axis=0, keepdims=True)
    gains = (route_scale * chosen / total).astype(bf16)
    before = (
        lax.broadcasted_iota(jnp.int32, (tok, tok), 0)
        < lax.broadcasted_iota(jnp.int32, (tok, tok), 1)
    ).astype(bf16)
    rank = jnp.dot(mask.astype(bf16), before, preferred_element_type=f32)
    rank = jnp.where(mask > 0, rank, -1.0)
    return mask, chosen, total, gains, rank


def body(grad_out, tokens, scores, expert_ids, hidden_act, down_weight):
    sources = lax.axis_size(AX)
    tok = expert_ids.shape[0]
    experts = scores.shape[1]
    slots = hidden_act.shape[1]
    most = slots // sources
    cols = grad_out.shape[1]
    mask, chosen, total, gains, rank = router(scores, expert_ids)
    place = jnp.stack([rank, gains.astype(f32)], axis=1)
    place = lax.all_to_all(place, AX, split_axis=0, concat_axis=0, tiled=True)
    every = lax.all_gather(grad_out, AX, axis=0, tiled=True).reshape(sources, tok, cols)
    rank_in, gain_in = place[:, 0], place[:, 1]
    hit = rank_in[:, None, :] == lax.broadcasted_iota(jnp.int32, (sources, most, tok), 1).astype(f32)
    pick = hit.astype(bf16)
    gain = jnp.sum(jnp.where(hit, gain_in[:, None, :], 0.0), axis=2).reshape(slots)
    rows = lax.dot_general(pick, every, (((2,), (1,)), ((0,), (0,))), preferred_element_type=f32)
    rows = rows.astype(bf16).reshape(slots, cols)
    scaled = (gain[:, None] * rows.astype(f32)).astype(bf16)
    hidden = hidden_act[0]
    down = down_weight[0]
    through = lax.dot_general(rows, down, (((1,), (1,)), ((), ())), preferred_element_type=f32)
    slot = jnp.sum(through * hidden.astype(f32), axis=1).reshape(sources, most)
    hidden_grad = lax.psum_scatter(
        (gain[:, None] * through).astype(bf16), "dp", scatter_dimension=0, tiled=True
    )[None]
    weight_grad = lax.dot_general(
        hidden, scaled, (((0,), (0,)), ((), ())), preferred_element_type=f32
    ).astype(bf16)[None]
    back = jnp.sum(jnp.where(hit, slot[:, :, None], 0.0), axis=1)
    both = lax.all_gather(back, "dp", axis=0)
    back = both[0] + both[1] if both.shape[0] == 2 else jnp.sum(both, axis=0)
    route = lax.all_to_all(back, AX, split_axis=0, concat_axis=0, tiled=True)
    mixed = jnp.sum(route * chosen, axis=0, keepdims=True) / total
    score_grad = route_scale / total * (route - mixed)
    logit_grad = (mask * score_grad * chosen * (1.0 - chosen)).astype(bf16)
    gate_part = jnp.dot(logit_grad, tokens, preferred_element_type=f32)
    gate_grad = lax.psum(gate_part, AX)
    return (weight_grad, hidden_grad, gate_grad)


def solution(mesh):
    return jax.shard_map(
        body,
        mesh=mesh,
        in_specs=(
            P(AX, "dp"),
            P(AX, "dp"),
            P(AX, None),
            P(AX, None),
            P(AX, None, None),
            P(AX, None, "dp"),
        ),
        out_specs=(P(AX, None, "dp"), P(AX, "dp", None), P(None, "dp")),
        check_vma=False,
    )
```

```python
import jax
import jax.numpy as jnp
from jax import lax
from jax.experimental import pallas as pl
from jax.experimental.pallas import tpu as pltpu
from jax.sharding import PartitionSpec as P
import functools

route_scale = 2.5
AX = ("ep", "node")
f32, bf16 = jnp.float32, jnp.bfloat16


def router(scores, expert_ids):
    tok = expert_ids.shape[0]
    experts = scores.shape[1]
    ids_t = expert_ids.T
    names = lax.broadcasted_iota(jnp.int32, (experts, tok), 0)
    mask = jnp.zeros((experts, tok), f32)
    for k in range(expert_ids.shape[1]):
        mask = mask + (ids_t[k][None, :] == names).astype(f32)
    chosen = mask * scores.T
    total = jnp.sum(chosen, axis=0, keepdims=True)
    gains = (route_scale * chosen / total).astype(bf16)
    before = (
        lax.broadcasted_iota(jnp.int32, (tok, tok), 0)
        < lax.broadcasted_iota(jnp.int32, (tok, tok), 1)
    ).astype(bf16)
    rank = jnp.dot(mask.astype(bf16), before, preferred_element_type=f32)
    rank = jnp.where(mask > 0, rank, -4096.0)
    return mask, chosen, total, gains, rank


MESH = pl.DeviceIdType.MESH
VM = pl.BlockSpec(memory_space=pltpu.VMEM)
ANY = pl.BlockSpec(memory_space=pl.ANY)


def gather_kernel(ep_n, inner, node_n, block, place, every, meta, local_sem,
                  send, recv, meta_send, meta_recv):
    outer = ep_n // inner
    ep, node = lax.axis_index("ep"), lax.axis_index("node")
    z, x = ep // inner, ep % inner
    n = ep_n * node_n
    me = ep * node_n + node

    def dev(zz, xx, cc):
        return {"ep": zz * inner + xx, "node": cc}

    def source(zz, xx, cc):
        return (zz * inner + xx) * node_n + cc

    barrier = pltpu.get_barrier_semaphore()

    def greet(j, carry):
        p = lax.rem(me + j, n)
        pl.semaphore_signal(barrier, inc=1, device_id={"ep": p // node_n, "node": p % node_n},
                            device_id_type=MESH)
        return carry

    lax.fori_loop(1, n, greet, 0)
    pl.semaphore_wait(barrier, n - 1)

    def push(way, s, to, own=False):
        pltpu.make_async_remote_copy(
            src_ref=block if own else every.at[s], dst_ref=every.at[s],
            send_sem=send.at[way, s], recv_sem=recv.at[s],
            device_id=to, device_id_type=MESH).start()

    def sent(way, s):
        pltpu.make_async_remote_copy(
            src_ref=every.at[s], dst_ref=every.at[s],
            send_sem=send.at[way, s], recv_sem=recv.at[s],
            device_id=dev(z, x, node), device_id_type=MESH).wait_send()

    def arrived(s):
        pltpu.make_async_remote_copy(
            src_ref=every.at[s], dst_ref=every.at[s],
            send_sem=send.at[0, s], recv_sem=recv.at[s],
            device_id=dev(z, x, node), device_id_type=MESH).wait_recv()

    def when(*conds):
        c = conds[0]
        for d in conds[1:]:
            c = jnp.logical_and(c, d)
        return pl.when(c)

    def start_x(s, up, down, own=False):
        @pl.when(up)
        def _():
            push(2, s, dev(z, x + 1, node), own)

        @pl.when(down)
        def _():
            push(3, s, dev(z, x - 1, node), own)

    def start_core(s, own=False):
        for k in range(1, node_n):
            push(3 + k, s, dev(z, x, lax.rem(node + k, node_n)), own)

    can_zu, can_zd = z + 1 < outer, z >= 1
    can_xu, can_xd = x + 1 < inner, x >= 1

    @pl.when(can_zu)
    def _():
        push(0, me, dev(z + 1, x, node), True)

    @pl.when(can_zd)
    def _():
        push(1, me, dev(z - 1, x, node), True)

    start_x(me, can_xu, can_xd, True)

    def tell(j, carry):
        p = lax.rem(me + j, n)
        pltpu.make_async_remote_copy(
            src_ref=place.at[p], dst_ref=meta.at[me],
            send_sem=meta_send.at[j], recv_sem=meta_recv.at[j],
            device_id={"ep": p // node_n, "node": p % node_n}, device_id_type=MESH).start()
        return carry

    lax.fori_loop(1, n, tell, 0)
    start_core(me, True)
    keep = pltpu.make_async_copy(block, every.at[me], local_sem)
    keep.start()
    meta[me] = place[me]

    def z_rows(t):
        if t == 0:
            return [(z >= 0, z, None)]
        return [(z >= t, z - t, True), (z + t < outer, z + t, False)]

    def x_step(t):
        for exists, row, _ in z_rows(t):
            for d in range(1, inner):
                s_low = source(row, x - d, node)
                s_high = source(row, x + d, node)

                @when(exists, x >= d)
                def _():
                    arrived(s_low)
                    start_core(s_low)

                    @pl.when(can_xu)
                    def _():
                        push(2, s_low, dev(z, x + 1, node))

                @when(exists, x + d < inner)
                def _():
                    arrived(s_high)
                    start_core(s_high)

                    @pl.when(can_xd)
                    def _():
                        push(3, s_high, dev(z, x - 1, node))

    for t in range(1, outer):
        for exists, row, below in z_rows(t):
            s = source(row, x, node)

            @pl.when(exists)
            def _():
                arrived(s)
                if below:
                    @pl.when(can_zu)
                    def _():
                        push(0, s, dev(z + 1, x, node))
                else:
                    @pl.when(can_zd)
                    def _():
                        push(1, s, dev(z - 1, x, node))
                start_x(s, can_xu, can_xd)
                start_core(s)
        x_step(t - 1)
    x_step(outer - 1)

    keep.wait()

    def rest(e, carry):
        for k in range(1, node_n):
            arrived(e * node_n + lax.rem(node + k, node_n))
        return carry

    lax.fori_loop(0, ep_n, rest, 0)

    def ended(e, carry):
        s = e * node_n + node
        row, col = e // inner, e % inner
        mine = col == x

        @when(mine, row <= z, can_zu)
        def _():
            sent(0, s)

        @when(mine, row >= z, can_zd)
        def _():
            sent(1, s)

        @when(col <= x, can_xu)
        def _():
            sent(2, s)

        @when(col >= x, can_xd)
        def _():
            sent(3, s)

        for k in range(1, node_n):
            sent(3 + k, s)
        return carry

    lax.fori_loop(0, ep_n, ended, 0)

    def told(j, carry):
        pltpu.make_async_remote_copy(
            src_ref=place.at[0], dst_ref=meta.at[0],
            send_sem=meta_send.at[j], recv_sem=meta_recv.at[j],
            device_id=dev(z, x, node), device_id_type=MESH).wait()
        return carry

    lax.fori_loop(1, n, told, 0)


def gather(ep_n, inner, node_n, grad_out, place):
    n = ep_n * node_n
    return pl.pallas_call(
        functools.partial(gather_kernel, ep_n, inner, node_n),
        out_shape=(jax.ShapeDtypeStruct((n,) + grad_out.shape, grad_out.dtype),
                   jax.ShapeDtypeStruct(place.shape, place.dtype)),
        in_specs=[ANY, VM],
        out_specs=(ANY, VM),
        scratch_shapes=[
            pltpu.SemaphoreType.DMA,
            pltpu.SemaphoreType.DMA((3 + node_n, n)),
            pltpu.SemaphoreType.DMA((n,)),
            pltpu.SemaphoreType.DMA((n,)),
            pltpu.SemaphoreType.DMA((n,)),
        ],
        compiler_params=pltpu.CompilerParams(collective_id=0, has_side_effects=True,
                                             vmem_limit_bytes=16 << 20),
        name="gather",
    )(grad_out, place)


def through_kernel(group, most, tok, every, meta, down, hidden, scaled, partial, back, pick, gain, total, plain):
    step, steps = pl.program_id(0), pl.num_programs(0)
    n = every.shape[0]
    rows = group * most

    def hits(g):
        for j in range(group):
            ranks = meta[g * group + j, 0:1, :]
            local = lax.broadcasted_iota(jnp.int32, (rows, tok), 0).astype(f32) - float(j * most)
            yield j, (ranks == local)

    @pl.when(step == 0)
    def _():
        total[...] = jnp.zeros_like(total)
        for g in range(n // group):
            own = jnp.zeros((rows, 1), f32)
            for j, hit in hits(g):
                own = own + jnp.sum(jnp.where(hit, meta[g * group + j, 1:2, :], 0.0), axis=1, keepdims=True)
                pick[g * group + j] = hit.astype(f32).astype(bf16)
            gain[g * rows:(g + 1) * rows, :] = own

    for g in range(n // group):
        got = jnp.zeros((rows, every.shape[2]), f32)
        for j in range(group):
            got = got + jnp.dot(pick[g * group + j], every[g * group + j], preferred_element_type=f32)
        span = slice(g * rows, (g + 1) * rows)
        scaled[span, :] = (got * gain[span, :]).astype(bf16)
        plain[span, :] = got.astype(bf16)
    total[...] += lax.dot_general(plain[...], down[...], (((1,), (1,)), ((), ())), preferred_element_type=f32)

    @pl.when(step == steps - 1)
    def _():
        for g in range(n // group):
            span = slice(g * rows, (g + 1) * rows)
            u = total[span, :]
            partial[span, :] = (gain[span, :] * u).astype(bf16)
            slot = jnp.sum(u * hidden[span, :].astype(f32), axis=1, keepdims=True)
            for j, hit in hits(g):
                back[g * group + j] = jnp.sum(jnp.where(hit, slot, 0.0), axis=0, keepdims=True)


def through(every, meta, down, hidden):
    n, tok, cols = every.shape
    slots, width = hidden.shape
    most = slots // n
    group = 1
    while (group * most) % 16:
        group *= 2
    part = 512
    return pl.pallas_call(
        functools.partial(through_kernel, group, most, tok),
        grid=(cols // part,),
        out_shape=(jax.ShapeDtypeStruct((slots, cols), bf16),
                   jax.ShapeDtypeStruct((slots, width), bf16),
                   jax.ShapeDtypeStruct((n, 1, tok), f32)),
        in_specs=[pl.BlockSpec((n, tok, part), lambda i: (0, 0, i)),
                  pl.BlockSpec((n, 2, tok), lambda i: (0, 0, 0)),
                  pl.BlockSpec((width, part), lambda i: (0, i)),
                  pl.BlockSpec((slots, width), lambda i: (0, 0))],
        out_specs=(pl.BlockSpec((slots, part), lambda i: (0, i)),
                   pl.BlockSpec((slots, width), lambda i: (0, 0)),
                   pl.BlockSpec((n, 1, tok), lambda i: (0, 0, 0))),
        scratch_shapes=[pltpu.VMEM((n, group * most, tok), bf16),
                        pltpu.VMEM((slots, 1), f32),
                        pltpu.VMEM((slots, width), f32),
                        pltpu.VMEM((slots, part), bf16)],
        compiler_params=pltpu.CompilerParams(vmem_limit_bytes=56 << 20),
        cost_estimate=pl.CostEstimate(flops=2 * slots * cols * (width + tok), transcendentals=0,
                                      bytes_accessed=2 * (n * tok * cols + 2 * slots * cols)),
        name="through",
    )(every, meta, down, hidden)


def weight_kernel(hidden, scaled, out, turned):
    @pl.when(pl.program_id(0) == 0)
    def _():
        turned[...] = hidden[...].T

    out[...] = jnp.dot(turned[...], scaled[...], preferred_element_type=f32).astype(bf16)


def weight(hidden, scaled):
    slots, width = hidden.shape
    cols = scaled.shape[1]
    part = 512
    return pl.pallas_call(
        weight_kernel,
        grid=(cols // part,),
        out_shape=jax.ShapeDtypeStruct((width, cols), bf16),
        in_specs=[pl.BlockSpec((slots, width), lambda i: (0, 0)),
                  pl.BlockSpec((slots, part), lambda i: (0, i))],
        out_specs=pl.BlockSpec((width, part), lambda i: (0, i)),
        scratch_shapes=[pltpu.VMEM((width, slots), bf16)],
        compiler_params=pltpu.CompilerParams(vmem_limit_bytes=48 << 20),
        cost_estimate=pl.CostEstimate(flops=2 * slots * cols * width, transcendentals=0,
                                      bytes_accessed=2 * (slots * cols + slots * width + cols * width)),
        name="weight",
    )(hidden, scaled)


def gate_kernel(ep_n, node_n, dp_n, back, mask, chosen, whole, tokens, out, home, part, inbox,
                home_send, home_recv, send_a, recv_a, send_b, recv_b):
    ep, node, dp = lax.axis_index("ep"), lax.axis_index("node"), lax.axis_index("dp")
    n = ep_n * node_n
    me = ep * node_n + node
    everyone = n * dp_n

    def at(p, q):
        return {"ep": p // node_n, "node": p % node_n, "dp": q}

    def peer(j):
        return lax.rem(me + j % n, n), lax.rem(dp + j // n, dp_n)

    barrier = pltpu.get_barrier_semaphore()

    def greet(j, carry):
        p, q = peer(j)
        pl.semaphore_signal(barrier, inc=1, device_id=at(p, q), device_id_type=MESH)
        return carry

    lax.fori_loop(1, everyone, greet, 0)
    pl.semaphore_wait(barrier, everyone - 1)

    def home_copy(j):
        p, q = peer(j)
        return pltpu.make_async_remote_copy(
            src_ref=back.at[p], dst_ref=home.at[dp, me],
            send_sem=home_send.at[j], recv_sem=home_recv.at[j],
            device_id=at(p, q), device_id_type=MESH)

    def go_home(j, carry):
        home_copy(j).start()
        return carry

    lax.fori_loop(1, everyone, go_home, 0)
    home[dp, me] = back[me]

    def came_home(j, carry):
        home_copy(j).wait()
        return carry

    lax.fori_loop(1, everyone, came_home, 0)
    route = home[0, :, 0, :]
    for q in range(1, dp_n):
        route = route + home[q, :, 0, :]
    picked = chosen[...]
    all_of = whole[...]
    mixed = jnp.sum(route * picked, axis=0, keepdims=True) / all_of
    score_grad = route_scale / all_of * (route - mixed)
    logit = (mask[...] * score_grad * picked * (1.0 - picked)).astype(bf16)
    lanes = part.shape[2]
    for i in range(part.shape[1]):
        part[:, i, :] = jnp.dot(logit, tokens[:, i * lanes:(i + 1) * lanes], preferred_element_type=f32)

    def to_owner(j):
        p = lax.rem(me + j, n)
        return pltpu.make_async_remote_copy(
            src_ref=part.at[p], dst_ref=inbox.at[j],
            send_sem=send_a.at[j], recv_sem=recv_a.at[j],
            device_id=at(p, dp), device_id_type=MESH)

    def start_a(j, carry):
        to_owner(j).start()
        return carry

    def wait_a(j, carry):
        to_owner(j).wait()
        return carry

    lax.fori_loop(1, n, start_a, 0)
    lax.fori_loop(1, n, wait_a, 0)
    out[me] = lax.fori_loop(1, n, lambda j, acc: acc + inbox[j], part[me])

    def spread(j):
        p = lax.rem(me + j, n)
        return pltpu.make_async_remote_copy(
            src_ref=out.at[me], dst_ref=out.at[me],
            send_sem=send_b.at[j], recv_sem=recv_b.at[j],
            device_id=at(p, dp), device_id_type=MESH)

    def start_b(j, carry):
        spread(j).start()
        return carry

    def wait_b(j, carry):
        spread(j).wait()
        return carry

    lax.fori_loop(1, n, start_b, 0)
    lax.fori_loop(1, n, wait_b, 0)


def gate(ep_n, node_n, dp_n, back, mask, chosen, total, tokens):
    n = ep_n * node_n
    tok, cols = tokens.shape
    lanes = 128
    shape = (n, cols // lanes, lanes)
    dma = pltpu.SemaphoreType.DMA
    return pl.pallas_call(
        functools.partial(gate_kernel, ep_n, node_n, dp_n),
        out_shape=jax.ShapeDtypeStruct(shape, f32),
        in_specs=[VM] * 5,
        out_specs=VM,
        scratch_shapes=[pltpu.VMEM((dp_n, n, 1, tok), f32),
                        pltpu.VMEM(shape, f32), pltpu.VMEM(shape, f32),
                        dma((n * dp_n,)), dma((n * dp_n,)),
                        dma((n,)), dma((n,)), dma((n,)), dma((n,))],
        compiler_params=pltpu.CompilerParams(collective_id=1, has_side_effects=True,
                                             vmem_limit_bytes=24 << 20),
        cost_estimate=pl.CostEstimate(flops=2 * tok * cols * n, transcendentals=0,
                                      bytes_accessed=8 * n * cols),
        name="gate",
    )(back, mask, chosen, total, tokens).reshape(n, cols)


def body(ep_n, node_n, dp_n, grad_out, tokens, scores, expert_ids, hidden_act, down_weight):
    inner = 2 if ep_n <= 8 else 8
    mask, chosen, total, gains, rank = router(scores, expert_ids)
    place = jnp.stack([rank, gains.astype(f32)], axis=1)
    every, meta = gather(ep_n, inner, node_n, grad_out, place)
    hidden = hidden_act[0]
    scaled, partial, back = through(every, meta, down_weight[0], hidden)
    hidden_grad = lax.psum_scatter(partial, "dp", scatter_dimension=0, tiled=True)[None]
    gate_grad = gate(ep_n, node_n, dp_n, back, mask, chosen, total, tokens)
    weight_grad = weight(hidden, scaled)[None]
    return (weight_grad, hidden_grad, gate_grad)


def solution(mesh):
    sizes = [mesh.shape[a] for a in ("ep", "node", "dp")]
    return jax.shard_map(
        functools.partial(body, *sizes),
        mesh=mesh,
        in_specs=(
            P(AX, "dp"),
            P(AX, "dp"),
            P(AX, None),
            P(AX, None),
            P(AX, None, None),
            P(AX, None, "dp"),
        ),
        out_specs=(P(AX, None, "dp"), P(AX, "dp", None), P(None, "dp")),
        check_vma=False,
    )
```

```python
import jax
import jax.numpy as jnp
from jax import lax
from jax.experimental import pallas as pl
from jax.experimental.pallas import tpu as pltpu
from jax.sharding import PartitionSpec as P
import functools

route_scale = 2.5
AX = ("ep", "node")
f32, bf16 = jnp.float32, jnp.bfloat16


def router(scores, expert_ids):
    tok = expert_ids.shape[0]
    experts = scores.shape[1]
    ids_t = expert_ids.T
    names = lax.broadcasted_iota(jnp.int32, (experts, tok), 0)
    mask = jnp.zeros((experts, tok), f32)
    for k in range(expert_ids.shape[1]):
        mask = mask + (ids_t[k][None, :] == names).astype(f32)
    chosen = mask * scores.T
    total = jnp.sum(chosen, axis=0, keepdims=True)
    gains = (route_scale * chosen / total).astype(bf16)
    before = (
        lax.broadcasted_iota(jnp.int32, (tok, tok), 0)
        < lax.broadcasted_iota(jnp.int32, (tok, tok), 1)
    ).astype(bf16)
    rank = jnp.dot(mask.astype(bf16), before, preferred_element_type=f32)
    rank = jnp.where(mask > 0, rank, -4096.0)
    return mask, chosen, total, gains, rank


MESH = pl.DeviceIdType.MESH
VM = pl.BlockSpec(memory_space=pltpu.VMEM)
ANY = pl.BlockSpec(memory_space=pl.ANY)


def gather_kernel(ep_n, inner, node_n, part, block, place, down_in, hidden_in,
                  every, scaled_out, partial_out, back,
                  meta, down, hidden, scaled, partial, held, acc, local_sem, load_sem, held_sem, out_sem,
                  send, recv, meta_send, meta_recv):
    outer = ep_n // inner
    ep, node = lax.axis_index("ep"), lax.axis_index("node")
    z, x = ep // inner, ep % inner
    n = ep_n * node_n
    me = ep * node_n + node

    def dev(zz, xx, cc):
        return {"ep": zz * inner + xx, "node": cc}

    def source(zz, xx, cc):
        return (zz * inner + xx) * node_n + cc

    load_down = pltpu.make_async_copy(down_in, down, load_sem.at[0])
    load_hidden = pltpu.make_async_copy(hidden_in, hidden, load_sem.at[1])
    load_down.start()
    load_hidden.start()
    barrier = pltpu.get_barrier_semaphore()

    def greet(j, carry):
        p = lax.rem(me + j, n)
        pl.semaphore_signal(barrier, inc=1, device_id={"ep": p // node_n, "node": p % node_n},
                            device_id_type=MESH)
        return carry

    lax.fori_loop(1, n, greet, 0)
    pl.semaphore_wait(barrier, n - 1)

    def push(way, s, to, own=False):
        pltpu.make_async_remote_copy(
            src_ref=block if own else every.at[s], dst_ref=every.at[s],
            send_sem=send.at[way, s], recv_sem=recv.at[s],
            device_id=to, device_id_type=MESH).start()

    def sent(way, s):
        pltpu.make_async_remote_copy(
            src_ref=every.at[s], dst_ref=every.at[s],
            send_sem=send.at[way, s], recv_sem=recv.at[s],
            device_id=dev(z, x, node), device_id_type=MESH).wait_send()

    def arrived(s):
        pltpu.make_async_remote_copy(
            src_ref=every.at[s], dst_ref=every.at[s],
            send_sem=send.at[0, s], recv_sem=recv.at[s],
            device_id=dev(z, x, node), device_id_type=MESH).wait_recv()

    def when(*conds):
        c = conds[0]
        for d in conds[1:]:
            c = jnp.logical_and(c, d)
        return pl.when(c)

    def start_x(s, up, down, own=False):
        @pl.when(up)
        def _():
            push(2, s, dev(z, x + 1, node), own)

        @pl.when(down)
        def _():
            push(3, s, dev(z, x - 1, node), own)

    def start_core(s, own=False):
        for k in range(1, node_n):
            push(3 + k, s, dev(z, x, lax.rem(node + k, node_n)), own)

    can_zu, can_zd = z + 1 < outer, z >= 1
    can_xu, can_xd = x + 1 < inner, x >= 1

    @pl.when(can_zu)
    def _():
        push(0, me, dev(z + 1, x, node), True)

    @pl.when(can_zd)
    def _():
        push(1, me, dev(z - 1, x, node), True)

    start_x(me, can_xu, can_xd, True)

    def tell(j, carry):
        p = lax.rem(me + j, n)
        pltpu.make_async_remote_copy(
            src_ref=place.at[p], dst_ref=meta.at[me],
            send_sem=meta_send.at[j], recv_sem=meta_recv.at[j],
            device_id={"ep": p // node_n, "node": p % node_n}, device_id_type=MESH).start()
        return carry

    lax.fori_loop(1, n, tell, 0)
    start_core(me, True)
    keep = pltpu.make_async_copy(block, every.at[me], local_sem)
    keep.start()
    meta[me] = place[me]

    def sides(t):
        return [(z >= t, z - t, True), (jnp.logical_and(t >= 1, z + t < outer), z + t, False)]

    slots = scaled.shape[1]
    tok, cols = held.shape

    def work(s):
        fetch = pltpu.make_async_copy(every.at[s], held, held_sem)
        fetch.start()
        spot = meta[s]
        hit = spot[0:1, :] == lax.broadcasted_iota(jnp.int32, (slots, tok), 0).astype(f32)
        gain = jnp.sum(jnp.where(hit, spot[1:2, :], 0.0), axis=1, keepdims=True)
        pick = hit.astype(f32).astype(bf16)
        acc[...] = jnp.zeros_like(acc)
        fetch.wait()

        def columns(i, carry):
            span = pl.ds(pl.multiple_of(i * part, part), part)
            got = jnp.dot(pick, held[:, span], preferred_element_type=f32)
            scaled[s, :, span] = (got * gain).astype(bf16)
            acc[...] += lax.dot_general(got.astype(bf16), down[:, span], (((1,), (1,)), ((), ())),
                                        preferred_element_type=f32)
            return carry

        lax.fori_loop(0, cols // part, columns, 0)
        u = acc[...]
        partial[s] = (gain * u).astype(bf16)
        slot = jnp.sum(u * hidden[s].astype(f32), axis=1, keepdims=True)
        back[s] = jnp.sum(jnp.where(hit, slot, 0.0), axis=0, keepdims=True)
        pltpu.make_async_copy(scaled.at[s], scaled_out.at[s], out_sem.at[0, s]).start()
        pltpu.make_async_copy(partial.at[s], partial_out.at[s], out_sem.at[1, s]).start()

    def told(j, carry):
        pltpu.make_async_remote_copy(
            src_ref=place.at[0], dst_ref=meta.at[0],
            send_sem=meta_send.at[j], recv_sem=meta_recv.at[j],
            device_id=dev(z, x, node), device_id_type=MESH).wait()
        return carry

    keep.wait()
    load_down.wait()
    load_hidden.wait()
    lax.fori_loop(1, n, told, 0)

    def step(t, carry):
        for exists, row, below in sides(t):
            s = source(row, x, node)

            @when(exists, t >= 1)
            def _():
                arrived(s)
                if below:
                    @pl.when(can_zu)
                    def _():
                        push(0, s, dev(z + 1, x, node))
                else:
                    @pl.when(can_zd)
                    def _():
                        push(1, s, dev(z - 1, x, node))
                start_x(s, can_xu, can_xd)
                start_core(s)

        for exists, row, _ in sides(t - 1):
            for far in range(1, inner):
                s_low = source(row, x - far, node)
                s_high = source(row, x + far, node)

                @when(exists, t >= 1, x >= far)
                def _():
                    arrived(s_low)
                    start_core(s_low)

                    @pl.when(can_xu)
                    def _():
                        push(2, s_low, dev(z, x + 1, node))

                @when(exists, t >= 1, x + far < inner)
                def _():
                    arrived(s_high)
                    start_core(s_high)

                    @pl.when(can_xd)
                    def _():
                        push(3, s_high, dev(z, x - 1, node))

        def each(i, carry):
            e, c = i % ep_n, lax.rem(node + i // ep_n, node_n)
            row, col = e // inner, e % inner
            away = jnp.abs(row - z) + jnp.where(col == x, 0, 1)
            s = e * node_n + c

            @pl.when(away == t)
            def _():
                @pl.when(c != node)
                def _():
                    arrived(s)

                work(s)
            return carry

        lax.fori_loop(0, n, each, 0)
        return carry

    lax.fori_loop(0, outer + 1, step, 0)

    def stored(s, carry):
        pltpu.make_async_copy(scaled.at[s], scaled_out.at[s], out_sem.at[0, s]).wait()
        pltpu.make_async_copy(partial.at[s], partial_out.at[s], out_sem.at[1, s]).wait()
        return carry

    lax.fori_loop(0, n, stored, 0)

    def ended(e, carry):
        s = e * node_n + node
        row, col = e // inner, e % inner
        mine = col == x

        @when(mine, row <= z, can_zu)
        def _():
            sent(0, s)

        @when(mine, row >= z, can_zd)
        def _():
            sent(1, s)

        @when(col <= x, can_xu)
        def _():
            sent(2, s)

        @when(col >= x, can_xd)
        def _():
            sent(3, s)

        for k in range(1, node_n):
            sent(3 + k, s)
        return carry

    lax.fori_loop(0, ep_n, ended, 0)


def gather(ep_n, inner, node_n, grad_out, place, down, hidden):
    n = ep_n * node_n
    tok, cols = grad_out.shape
    width = down.shape[0]
    slots = hidden.shape[1]
    part = 512 if cols % 512 == 0 else cols
    dma = pltpu.SemaphoreType.DMA
    return pl.pallas_call(
        functools.partial(gather_kernel, ep_n, inner, node_n, part),
        out_shape=(jax.ShapeDtypeStruct((n, tok, cols), bf16),
                   jax.ShapeDtypeStruct((n, slots, cols), bf16),
                   jax.ShapeDtypeStruct((n, slots, width), bf16),
                   jax.ShapeDtypeStruct((n, 1, tok), f32)),
        in_specs=[ANY, VM, ANY, ANY],
        out_specs=(ANY, ANY, ANY, VM),
        scratch_shapes=[
            pltpu.VMEM(place.shape, f32), pltpu.VMEM((width, cols), bf16),
            pltpu.VMEM((n, slots, width), bf16), pltpu.VMEM((n, slots, cols), bf16),
            pltpu.VMEM((n, slots, width), bf16), pltpu.VMEM((tok, cols), bf16),
            pltpu.VMEM((slots, width), f32),
            dma, dma((2,)), dma, dma((2, n)),
            dma((3 + node_n, n)), dma((n,)), dma((n,)), dma((n,)),
        ],
        compiler_params=pltpu.CompilerParams(collective_id=0, has_side_effects=True,
                                             vmem_limit_bytes=56 << 20),
        name="gather",
    )(grad_out, place, down, hidden)


def weight_kernel(hidden, scaled, out, turned):
    @pl.when(pl.program_id(0) == 0)
    def _():
        turned[...] = hidden[...].T

    out[...] = jnp.dot(turned[...], scaled[...], preferred_element_type=f32).astype(bf16)


def weight(hidden, scaled):
    slots, width = hidden.shape
    cols = scaled.shape[1]
    part = 512 if cols % 512 == 0 else cols
    return pl.pallas_call(
        weight_kernel,
        grid=(cols // part,),
        out_shape=jax.ShapeDtypeStruct((width, cols), bf16),
        in_specs=[pl.BlockSpec((slots, width), lambda i: (0, 0)),
                  pl.BlockSpec((slots, part), lambda i: (0, i))],
        out_specs=pl.BlockSpec((width, part), lambda i: (0, i)),
        scratch_shapes=[pltpu.VMEM((width, slots), bf16)],
        compiler_params=pltpu.CompilerParams(vmem_limit_bytes=48 << 20),
        cost_estimate=pl.CostEstimate(flops=2 * slots * cols * width, transcendentals=0,
                                      bytes_accessed=2 * (slots * cols + slots * width + cols * width)),
        name="weight",
    )(hidden, scaled)


def gate_kernel(ep_n, node_n, dp_n, back, mask, chosen, whole, tokens, out, home, part, inbox,
                home_send, home_recv, send_a, recv_a, send_b, recv_b):
    ep, node, dp = lax.axis_index("ep"), lax.axis_index("node"), lax.axis_index("dp")
    n = ep_n * node_n
    me = ep * node_n + node
    everyone = n * dp_n

    def at(p, q):
        return {"ep": p // node_n, "node": p % node_n, "dp": q}

    def peer(j):
        return lax.rem(me + j % n, n), lax.rem(dp + j // n, dp_n)

    barrier = pltpu.get_barrier_semaphore()

    def greet(j, carry):
        p, q = peer(j)
        pl.semaphore_signal(barrier, inc=1, device_id=at(p, q), device_id_type=MESH)
        return carry

    lax.fori_loop(1, everyone, greet, 0)
    pl.semaphore_wait(barrier, everyone - 1)

    def home_copy(j):
        p, q = peer(j)
        return pltpu.make_async_remote_copy(
            src_ref=back.at[p], dst_ref=home.at[dp, me],
            send_sem=home_send.at[j], recv_sem=home_recv.at[j],
            device_id=at(p, q), device_id_type=MESH)

    def go_home(j, carry):
        home_copy(j).start()
        return carry

    lax.fori_loop(1, everyone, go_home, 0)
    home[dp, me] = back[me]

    def came_home(j, carry):
        home_copy(j).wait()
        return carry

    lax.fori_loop(1, everyone, came_home, 0)
    route = home[0, :, 0, :]
    for q in range(1, dp_n):
        route = route + home[q, :, 0, :]
    picked = chosen[...]
    all_of = whole[...]
    mixed = jnp.sum(route * picked, axis=0, keepdims=True) / all_of
    score_grad = route_scale / all_of * (route - mixed)
    logit = (mask[...] * score_grad * picked * (1.0 - picked)).astype(bf16)
    lanes = part.shape[2]
    for i in range(part.shape[1]):
        part[:, i, :] = jnp.dot(logit, tokens[:, i * lanes:(i + 1) * lanes], preferred_element_type=f32)

    def to_owner(j):
        p = lax.rem(me + j, n)
        return pltpu.make_async_remote_copy(
            src_ref=part.at[p], dst_ref=inbox.at[j],
            send_sem=send_a.at[j], recv_sem=recv_a.at[j],
            device_id=at(p, dp), device_id_type=MESH)

    def start_a(j, carry):
        to_owner(j).start()
        return carry

    def wait_a(j, carry):
        to_owner(j).wait()
        return carry

    lax.fori_loop(1, n, start_a, 0)
    lax.fori_loop(1, n, wait_a, 0)
    out[me] = lax.fori_loop(1, n, lambda j, acc: acc + inbox[j], part[me])

    def spread(j):
        p = lax.rem(me + j, n)
        return pltpu.make_async_remote_copy(
            src_ref=out.at[me], dst_ref=out.at[me],
            send_sem=send_b.at[j], recv_sem=recv_b.at[j],
            device_id=at(p, dp), device_id_type=MESH)

    def start_b(j, carry):
        spread(j).start()
        return carry

    def wait_b(j, carry):
        spread(j).wait()
        return carry

    lax.fori_loop(1, n, start_b, 0)
    lax.fori_loop(1, n, wait_b, 0)


def gate(ep_n, node_n, dp_n, back, mask, chosen, total, tokens):
    n = ep_n * node_n
    tok, cols = tokens.shape
    lanes = 128
    shape = (n, cols // lanes, lanes)
    dma = pltpu.SemaphoreType.DMA
    return pl.pallas_call(
        functools.partial(gate_kernel, ep_n, node_n, dp_n),
        out_shape=jax.ShapeDtypeStruct(shape, f32),
        in_specs=[VM] * 5,
        out_specs=VM,
        scratch_shapes=[pltpu.VMEM((dp_n, n, 1, tok), f32),
                        pltpu.VMEM(shape, f32), pltpu.VMEM(shape, f32),
                        dma((n * dp_n,)), dma((n * dp_n,)),
                        dma((n,)), dma((n,)), dma((n,)), dma((n,))],
        compiler_params=pltpu.CompilerParams(collective_id=1, has_side_effects=True,
                                             vmem_limit_bytes=24 << 20),
        cost_estimate=pl.CostEstimate(flops=2 * tok * cols * n, transcendentals=0,
                                      bytes_accessed=8 * n * cols),
        name="gate",
    )(back, mask, chosen, total, tokens).reshape(n, cols)


def body(ep_n, node_n, dp_n, grad_out, tokens, scores, expert_ids, hidden_act, down_weight):
    inner = 2 if ep_n <= 8 else 8
    mask, chosen, total, gains, rank = router(scores, expert_ids)
    place = jnp.stack([rank, gains.astype(f32)], axis=1)
    n = ep_n * node_n
    hidden = hidden_act[0]
    slots, width = hidden.shape
    most = slots // n
    fill = -most % 16
    apart = jnp.pad(hidden.reshape(n, most, width), ((0, 0), (0, fill), (0, 0)))
    every, scaled, partial, back = gather(ep_n, inner, node_n, grad_out, place, down_weight[0], apart)
    scaled = scaled[:, :most].reshape(slots, -1)
    partial = partial[:, :most].reshape(slots, width)
    hidden_grad = lax.psum_scatter(partial, "dp", scatter_dimension=0, tiled=True)[None]
    gate_grad = gate(ep_n, node_n, dp_n, back, mask, chosen, total, tokens)
    weight_grad = weight(hidden, scaled)[None]
    return (weight_grad, hidden_grad, gate_grad)


def solution(mesh):
    sizes = [mesh.shape[a] for a in ("ep", "node", "dp")]
    return jax.shard_map(
        functools.partial(body, *sizes),
        mesh=mesh,
        in_specs=(
            P(AX, "dp"),
            P(AX, "dp"),
            P(AX, None),
            P(AX, None),
            P(AX, None, None),
            P(AX, None, "dp"),
        ),
        out_specs=(P(AX, None, "dp"), P(AX, "dp", None), P(None, "dp")),
        check_vma=False,
    )
```

```python
import jax
import jax.numpy as jnp
from jax import lax
from jax.experimental import pallas as pl
from jax.experimental.pallas import tpu as pltpu
from jax.sharding import PartitionSpec as P
import functools

route_scale = 2.5
AX = ("ep", "node")
f32, bf16 = jnp.float32, jnp.bfloat16


def router(scores, expert_ids):
    tok = expert_ids.shape[0]
    experts = scores.shape[1]
    ids_t = expert_ids.T
    names = lax.broadcasted_iota(jnp.int32, (experts, tok), 0)
    mask = jnp.zeros((experts, tok), f32)
    for k in range(expert_ids.shape[1]):
        mask = mask + (ids_t[k][None, :] == names).astype(f32)
    chosen = mask * scores.T
    total = jnp.sum(chosen, axis=0, keepdims=True)
    gains = (route_scale * chosen / total).astype(bf16)
    before = (
        lax.broadcasted_iota(jnp.int32, (tok, tok), 0)
        < lax.broadcasted_iota(jnp.int32, (tok, tok), 1)
    ).astype(bf16)
    rank = jnp.dot(mask.astype(bf16), before, preferred_element_type=f32)
    rank = jnp.where(mask > 0, rank, -4096.0)
    return mask, chosen, total, gains, rank


MESH = pl.DeviceIdType.MESH
VM = pl.BlockSpec(memory_space=pltpu.VMEM)
ANY = pl.BlockSpec(memory_space=pl.ANY)


def gather_kernel(ep_n, inner, node_n, part, block, place, down_in, hidden_in,
                  every, scaled_out, partial_out, back,
                  meta, down, turned, hidden, scaled, partial, held, acc, local_sem, load_sem, held_sem, out_sem,
                  send, recv, meta_send, meta_recv):
    outer = ep_n // inner
    ep, node = lax.axis_index("ep"), lax.axis_index("node")
    z, x = ep // inner, ep % inner
    n = ep_n * node_n
    me = ep * node_n + node

    def dev(zz, xx, cc):
        return {"ep": zz * inner + xx, "node": cc}

    def source(zz, xx, cc):
        return (zz * inner + xx) * node_n + cc

    load_down = pltpu.make_async_copy(down_in, down, load_sem.at[0])
    load_hidden = pltpu.make_async_copy(hidden_in, hidden, load_sem.at[1])
    load_down.start()
    load_hidden.start()
    barrier = pltpu.get_barrier_semaphore()

    def greet(j, carry):
        p = lax.rem(me + j, n)
        pl.semaphore_signal(barrier, inc=1, device_id={"ep": p // node_n, "node": p % node_n},
                            device_id_type=MESH)
        return carry

    lax.fori_loop(1, n, greet, 0)
    pl.semaphore_wait(barrier, n - 1)

    def push(way, s, to, own=False):
        pltpu.make_async_remote_copy(
            src_ref=block if own else every.at[s], dst_ref=every.at[s],
            send_sem=send.at[way, s], recv_sem=recv.at[s],
            device_id=to, device_id_type=MESH).start()

    def sent(way, s):
        pltpu.make_async_remote_copy(
            src_ref=every.at[s], dst_ref=every.at[s],
            send_sem=send.at[way, s], recv_sem=recv.at[s],
            device_id=dev(z, x, node), device_id_type=MESH).wait_send()

    def arrived(s):
        pltpu.make_async_remote_copy(
            src_ref=every.at[s], dst_ref=every.at[s],
            send_sem=send.at[0, s], recv_sem=recv.at[s],
            device_id=dev(z, x, node), device_id_type=MESH).wait_recv()

    def when(*conds):
        c = conds[0]
        for d in conds[1:]:
            c = jnp.logical_and(c, d)
        return pl.when(c)

    def start_x(s, up, down, own=False):
        @pl.when(up)
        def _():
            push(2, s, dev(z, x + 1, node), own)

        @pl.when(down)
        def _():
            push(3, s, dev(z, x - 1, node), own)

    def start_core(s, own=False):
        for k in range(1, node_n):
            push(3 + k, s, dev(z, x, lax.rem(node + k, node_n)), own)

    can_zu, can_zd = z + 1 < outer, z >= 1
    can_xu, can_xd = x + 1 < inner, x >= 1

    @pl.when(can_zu)
    def _():
        push(0, me, dev(z + 1, x, node), True)

    @pl.when(can_zd)
    def _():
        push(1, me, dev(z - 1, x, node), True)

    start_x(me, can_xu, can_xd, True)

    def tell(j, carry):
        p = lax.rem(me + j, n)
        pltpu.make_async_remote_copy(
            src_ref=place.at[p], dst_ref=meta.at[me],
            send_sem=meta_send.at[j], recv_sem=meta_recv.at[j],
            device_id={"ep": p // node_n, "node": p % node_n}, device_id_type=MESH).start()
        return carry

    lax.fori_loop(1, n, tell, 0)
    start_core(me, True)
    keep = pltpu.make_async_copy(block, every.at[me], local_sem)
    keep.start()
    meta[me] = place[me]

    def sides(t):
        return [(z >= t, z - t, True), (jnp.logical_and(t >= 1, z + t < outer), z + t, False)]

    slots = scaled.shape[1]
    tok, cols = held.shape[1:]

    def turn(i, carry):
        span = pl.ds(pl.multiple_of(i * part, part), part)
        turned[span, :] = down[:, span].T
        return carry

    def work(e):
        own = range(node_n)
        fetch = [pltpu.make_async_copy(every.at[e * node_n + c], held.at[c], held_sem.at[c]) for c in own]
        for one in fetch:
            one.start()
        spots = [meta[e * node_n + c] for c in own]
        names = lax.broadcasted_iota(jnp.int32, (slots, tok), 0).astype(f32)
        hits = [spot[0:1, :] == names for spot in spots]
        gains = [jnp.sum(jnp.where(hits[c], spots[c][1:2, :], 0.0), axis=1, keepdims=True) for c in own]
        picks = [hit.astype(f32).astype(bf16) for hit in hits]
        acc[...] = jnp.zeros_like(acc)
        for one in fetch:
            one.wait()

        def columns(i, carry):
            span = pl.ds(pl.multiple_of(i * part, part), part)
            got = [jnp.dot(picks[c], held[c, :, span], preferred_element_type=f32) for c in own]
            for c in own:
                scaled[e * node_n + c, :, span] = (got[c] * gains[c]).astype(bf16)
            acc[...] += jnp.dot(jnp.concatenate(got, axis=0).astype(bf16), turned[span, :],
                                preferred_element_type=f32)
            return carry

        lax.fori_loop(0, cols // part, columns, 0)
        for c in own:
            s = e * node_n + c
            u = acc[c * slots:(c + 1) * slots, :]
            partial[s] = (gains[c] * u).astype(bf16)
            slot = jnp.sum(u * hidden[s].astype(f32), axis=1, keepdims=True)
            back[s] = jnp.sum(jnp.where(hits[c], slot, 0.0), axis=0, keepdims=True)
            pltpu.make_async_copy(scaled.at[s], scaled_out.at[s], out_sem.at[0, s]).start()
            pltpu.make_async_copy(partial.at[s], partial_out.at[s], out_sem.at[1, s]).start()

    def told(j, carry):
        pltpu.make_async_remote_copy(
            src_ref=place.at[0], dst_ref=meta.at[0],
            send_sem=meta_send.at[j], recv_sem=meta_recv.at[j],
            device_id=dev(z, x, node), device_id_type=MESH).wait()
        return carry

    keep.wait()
    load_down.wait()
    load_hidden.wait()
    lax.fori_loop(0, cols // part, turn, 0)
    lax.fori_loop(1, n, told, 0)

    def step(t, carry):
        for exists, row, below in sides(t):
            s = source(row, x, node)

            @when(exists, t >= 1)
            def _():
                arrived(s)
                if below:
                    @pl.when(can_zu)
                    def _():
                        push(0, s, dev(z + 1, x, node))
                else:
                    @pl.when(can_zd)
                    def _():
                        push(1, s, dev(z - 1, x, node))
                start_x(s, can_xu, can_xd)
                start_core(s)

        for exists, row, _ in sides(t - 1):
            for far in range(1, inner):
                s_low = source(row, x - far, node)
                s_high = source(row, x + far, node)

                @when(exists, t >= 1, x >= far)
                def _():
                    arrived(s_low)
                    start_core(s_low)

                    @pl.when(can_xu)
                    def _():
                        push(2, s_low, dev(z, x + 1, node))

                @when(exists, t >= 1, x + far < inner)
                def _():
                    arrived(s_high)
                    start_core(s_high)

                    @pl.when(can_xd)
                    def _():
                        push(3, s_high, dev(z, x - 1, node))

        def each(e, carry):
            row, col = e // inner, e % inner
            away = jnp.abs(row - z) + jnp.where(col == x, 0, 1)

            @pl.when(away == t)
            def _():
                for k in range(1, node_n):
                    arrived(e * node_n + lax.rem(node + k, node_n))
                work(e)
            return carry

        lax.fori_loop(0, ep_n, each, 0)
        return carry

    lax.fori_loop(0, outer + 1, step, 0)

    def stored(s, carry):
        pltpu.make_async_copy(scaled.at[s], scaled_out.at[s], out_sem.at[0, s]).wait()
        pltpu.make_async_copy(partial.at[s], partial_out.at[s], out_sem.at[1, s]).wait()
        return carry

    lax.fori_loop(0, n, stored, 0)

    def ended(e, carry):
        s = e * node_n + node
        row, col = e // inner, e % inner
        mine = col == x

        @when(mine, row <= z, can_zu)
        def _():
            sent(0, s)

        @when(mine, row >= z, can_zd)
        def _():
            sent(1, s)

        @when(col <= x, can_xu)
        def _():
            sent(2, s)

        @when(col >= x, can_xd)
        def _():
            sent(3, s)

        for k in range(1, node_n):
            sent(3 + k, s)
        return carry

    lax.fori_loop(0, ep_n, ended, 0)


def gather(ep_n, inner, node_n, grad_out, place, down, hidden):
    n = ep_n * node_n
    tok, cols = grad_out.shape
    width = down.shape[0]
    slots = hidden.shape[1]
    part = 512 if cols % 512 == 0 else cols
    dma = pltpu.SemaphoreType.DMA
    return pl.pallas_call(
        functools.partial(gather_kernel, ep_n, inner, node_n, part),
        out_shape=(jax.ShapeDtypeStruct((n, tok, cols), bf16),
                   jax.ShapeDtypeStruct((n, slots, cols), bf16),
                   jax.ShapeDtypeStruct((n, slots, width), bf16),
                   jax.ShapeDtypeStruct((n, 1, tok), f32)),
        in_specs=[ANY, VM, ANY, ANY],
        out_specs=(ANY, ANY, ANY, VM),
        scratch_shapes=[
            pltpu.VMEM(place.shape, f32), pltpu.VMEM((width, cols), bf16),
            pltpu.VMEM((cols, width), bf16),
            pltpu.VMEM((n, slots, width), bf16), pltpu.VMEM((n, slots, cols), bf16),
            pltpu.VMEM((n, slots, width), bf16), pltpu.VMEM((node_n, tok, cols), bf16),
            pltpu.VMEM((node_n * slots, width), f32),
            dma, dma((2,)), dma((node_n,)), dma((2, n)),
            dma((3 + node_n, n)), dma((n,)), dma((n,)), dma((n,)),
        ],
        compiler_params=pltpu.CompilerParams(collective_id=0, has_side_effects=True,
                                             vmem_limit_bytes=56 << 20),
        name="gather",
    )(grad_out, place, down, hidden)


def weight_kernel(hidden, scaled, out, turned):
    @pl.when(pl.program_id(0) == 0)
    def _():
        turned[...] = hidden[...].T

    out[...] = jnp.dot(turned[...], scaled[...], preferred_element_type=f32).astype(bf16)


def weight(hidden, scaled):
    slots, width = hidden.shape
    cols = scaled.shape[1]
    part = 512 if cols % 512 == 0 else cols
    return pl.pallas_call(
        weight_kernel,
        grid=(cols // part,),
        out_shape=jax.ShapeDtypeStruct((width, cols), bf16),
        in_specs=[pl.BlockSpec((slots, width), lambda i: (0, 0)),
                  pl.BlockSpec((slots, part), lambda i: (0, i))],
        out_specs=pl.BlockSpec((width, part), lambda i: (0, i)),
        scratch_shapes=[pltpu.VMEM((width, slots), bf16)],
        compiler_params=pltpu.CompilerParams(vmem_limit_bytes=48 << 20),
        cost_estimate=pl.CostEstimate(flops=2 * slots * cols * width, transcendentals=0,
                                      bytes_accessed=2 * (slots * cols + slots * width + cols * width)),
        name="weight",
    )(hidden, scaled)


def gate_kernel(ep_n, node_n, dp_n, back, mask, chosen, whole, tokens, out, home, part, inbox,
                home_send, home_recv, send_a, recv_a, send_b, recv_b):
    ep, node, dp = lax.axis_index("ep"), lax.axis_index("node"), lax.axis_index("dp")
    n = ep_n * node_n
    me = ep * node_n + node
    everyone = n * dp_n

    def at(p, q):
        return {"ep": p // node_n, "node": p % node_n, "dp": q}

    def peer(j):
        return lax.rem(me + j % n, n), lax.rem(dp + j // n, dp_n)

    barrier = pltpu.get_barrier_semaphore()

    def greet(j, carry):
        p, q = peer(j)
        pl.semaphore_signal(barrier, inc=1, device_id=at(p, q), device_id_type=MESH)
        return carry

    lax.fori_loop(1, everyone, greet, 0)
    pl.semaphore_wait(barrier, everyone - 1)

    def home_copy(j):
        p, q = peer(j)
        return pltpu.make_async_remote_copy(
            src_ref=back.at[p], dst_ref=home.at[dp, me],
            send_sem=home_send.at[j], recv_sem=home_recv.at[j],
            device_id=at(p, q), device_id_type=MESH)

    def go_home(j, carry):
        home_copy(j).start()
        return carry

    lax.fori_loop(1, everyone, go_home, 0)
    home[dp, me] = back[me]

    def came_home(j, carry):
        home_copy(j).wait()
        return carry

    lax.fori_loop(1, everyone, came_home, 0)
    route = home[0, :, 0, :]
    for q in range(1, dp_n):
        route = route + home[q, :, 0, :]
    picked = chosen[...]
    all_of = whole[...]
    mixed = jnp.sum(route * picked, axis=0, keepdims=True) / all_of
    score_grad = route_scale / all_of * (route - mixed)
    logit = (mask[...] * score_grad * picked * (1.0 - picked)).astype(bf16)
    lanes = part.shape[2]
    for i in range(part.shape[1]):
        part[:, i, :] = jnp.dot(logit, tokens[:, i * lanes:(i + 1) * lanes], preferred_element_type=f32)

    def to_owner(j):
        p = lax.rem(me + j, n)
        return pltpu.make_async_remote_copy(
            src_ref=part.at[p], dst_ref=inbox.at[j],
            send_sem=send_a.at[j], recv_sem=recv_a.at[j],
            device_id=at(p, dp), device_id_type=MESH)

    def start_a(j, carry):
        to_owner(j).start()
        return carry

    def wait_a(j, carry):
        to_owner(j).wait()
        return carry

    lax.fori_loop(1, n, start_a, 0)
    lax.fori_loop(1, n, wait_a, 0)
    out[me] = lax.fori_loop(1, n, lambda j, acc: acc + inbox[j], part[me])

    def spread(j):
        p = lax.rem(me + j, n)
        return pltpu.make_async_remote_copy(
            src_ref=out.at[me], dst_ref=out.at[me],
            send_sem=send_b.at[j], recv_sem=recv_b.at[j],
            device_id=at(p, dp), device_id_type=MESH)

    def start_b(j, carry):
        spread(j).start()
        return carry

    def wait_b(j, carry):
        spread(j).wait()
        return carry

    lax.fori_loop(1, n, start_b, 0)
    lax.fori_loop(1, n, wait_b, 0)


def gate(ep_n, node_n, dp_n, back, mask, chosen, total, tokens):
    n = ep_n * node_n
    tok, cols = tokens.shape
    lanes = 128
    shape = (n, cols // lanes, lanes)
    dma = pltpu.SemaphoreType.DMA
    return pl.pallas_call(
        functools.partial(gate_kernel, ep_n, node_n, dp_n),
        out_shape=jax.ShapeDtypeStruct(shape, f32),
        in_specs=[VM] * 5,
        out_specs=VM,
        scratch_shapes=[pltpu.VMEM((dp_n, n, 1, tok), f32),
                        pltpu.VMEM(shape, f32), pltpu.VMEM(shape, f32),
                        dma((n * dp_n,)), dma((n * dp_n,)),
                        dma((n,)), dma((n,)), dma((n,)), dma((n,))],
        compiler_params=pltpu.CompilerParams(collective_id=1, has_side_effects=True,
                                             vmem_limit_bytes=24 << 20),
        cost_estimate=pl.CostEstimate(flops=2 * tok * cols * n, transcendentals=0,
                                      bytes_accessed=8 * n * cols),
        name="gate",
    )(back, mask, chosen, total, tokens).reshape(n, cols)


def body(ep_n, node_n, dp_n, grad_out, tokens, scores, expert_ids, hidden_act, down_weight):
    inner = 2 if ep_n <= 8 else 8
    mask, chosen, total, gains, rank = router(scores, expert_ids)
    place = jnp.stack([rank, gains.astype(f32)], axis=1)
    n = ep_n * node_n
    hidden = hidden_act[0]
    slots, width = hidden.shape
    most = slots // n
    fill = -most % 16
    apart = jnp.pad(hidden.reshape(n, most, width), ((0, 0), (0, fill), (0, 0)))
    every, scaled, partial, back = gather(ep_n, inner, node_n, grad_out, place, down_weight[0], apart)
    scaled = scaled[:, :most].reshape(slots, -1)
    partial = partial[:, :most].reshape(slots, width)
    hidden_grad = lax.psum_scatter(partial, "dp", scatter_dimension=0, tiled=True)[None]
    gate_grad = gate(ep_n, node_n, dp_n, back, mask, chosen, total, tokens)
    weight_grad = weight(hidden, scaled)[None]
    return (weight_grad, hidden_grad, gate_grad)


def solution(mesh):
    sizes = [mesh.shape[a] for a in ("ep", "node", "dp")]
    return jax.shard_map(
        functools.partial(body, *sizes),
        mesh=mesh,
        in_specs=(
            P(AX, "dp"),
            P(AX, "dp"),
            P(AX, None),
            P(AX, None),
            P(AX, None, None),
            P(AX, None, "dp"),
        ),
        out_specs=(P(AX, None, "dp"), P(AX, "dp", None), P(None, "dp")),
        check_vma=False,
    )
```

```python
import jax
import jax.numpy as jnp
from jax import lax
from jax.experimental import pallas as pl
from jax.experimental.pallas import tpu as pltpu
from jax.sharding import PartitionSpec as P
import functools

route_scale = 2.5
AX = ("ep", "node")
f32, bf16 = jnp.float32, jnp.bfloat16


def router(scores, expert_ids):
    tok = expert_ids.shape[0]
    experts = scores.shape[1]
    ids_t = expert_ids.T
    names = lax.broadcasted_iota(jnp.int32, (experts, tok), 0)
    mask = jnp.zeros((experts, tok), f32)
    for k in range(expert_ids.shape[1]):
        mask = mask + (ids_t[k][None, :] == names).astype(f32)
    chosen = mask * scores.T
    total = jnp.sum(chosen, axis=0, keepdims=True)
    gains = (route_scale * chosen / total).astype(bf16)
    before = (
        lax.broadcasted_iota(jnp.int32, (tok, tok), 0)
        < lax.broadcasted_iota(jnp.int32, (tok, tok), 1)
    ).astype(bf16)
    rank = jnp.dot(mask.astype(bf16), before, preferred_element_type=f32)
    rank = jnp.where(mask > 0, rank, -4096.0)
    return mask, chosen, total, gains, rank


MESH = pl.DeviceIdType.MESH
VM = pl.BlockSpec(memory_space=pltpu.VMEM)
ANY = pl.BlockSpec(memory_space=pl.ANY)


def gather_kernel(ep_n, inner, node_n, part, block, place, down_in, hidden_in,
                  every, scaled_out, partial_out, back,
                  meta, down, turned, hidden, scaled, partial, held, acc, local_sem, load_sem, held_sem, out_sem,
                  send, recv, meta_send, meta_recv):
    outer = ep_n // inner
    ep, node = lax.axis_index("ep"), lax.axis_index("node")
    z, x = ep // inner, ep % inner
    n = ep_n * node_n
    me = ep * node_n + node

    def dev(zz, xx, cc):
        return {"ep": zz * inner + xx, "node": cc}

    def source(zz, xx, cc):
        return (zz * inner + xx) * node_n + cc

    load_down = pltpu.make_async_copy(down_in, down, load_sem.at[0])
    load_hidden = pltpu.make_async_copy(hidden_in, hidden, load_sem.at[1])
    load_down.start()
    load_hidden.start()
    barrier = pltpu.get_barrier_semaphore()

    def greet(j, carry):
        p = lax.rem(me + j, n)
        pl.semaphore_signal(barrier, inc=1, device_id={"ep": p // node_n, "node": p % node_n},
                            device_id_type=MESH)
        return carry

    lax.fori_loop(1, n, greet, 0)
    pl.semaphore_wait(barrier, n - 1)

    def push(way, s, to, own=False):
        pltpu.make_async_remote_copy(
            src_ref=block if own else every.at[s], dst_ref=every.at[s],
            send_sem=send.at[way, s], recv_sem=recv.at[s],
            device_id=to, device_id_type=MESH).start()

    def sent(way, s):
        pltpu.make_async_remote_copy(
            src_ref=every.at[s], dst_ref=every.at[s],
            send_sem=send.at[way, s], recv_sem=recv.at[s],
            device_id=dev(z, x, node), device_id_type=MESH).wait_send()

    def arrived(s):
        pltpu.make_async_remote_copy(
            src_ref=every.at[s], dst_ref=every.at[s],
            send_sem=send.at[0, s], recv_sem=recv.at[s],
            device_id=dev(z, x, node), device_id_type=MESH).wait_recv()

    def when(*conds):
        c = conds[0]
        for d in conds[1:]:
            c = jnp.logical_and(c, d)
        return pl.when(c)

    def start_x(s, up, down, own=False):
        @pl.when(up)
        def _():
            push(2, s, dev(z, x + 1, node), own)

        @pl.when(down)
        def _():
            push(3, s, dev(z, x - 1, node), own)

    def start_core(s, own=False):
        for k in range(1, node_n):
            push(3 + k, s, dev(z, x, lax.rem(node + k, node_n)), own)

    can_zu, can_zd = z + 1 < outer, z >= 1
    can_xu, can_xd = x + 1 < inner, x >= 1

    @pl.when(can_zu)
    def _():
        push(0, me, dev(z + 1, x, node), True)

    @pl.when(can_zd)
    def _():
        push(1, me, dev(z - 1, x, node), True)

    start_x(me, can_xu, can_xd, True)

    def tell(j, carry):
        p = lax.rem(me + j, n)
        pltpu.make_async_remote_copy(
            src_ref=place.at[p], dst_ref=meta.at[me],
            send_sem=meta_send.at[j], recv_sem=meta_recv.at[j],
            device_id={"ep": p // node_n, "node": p % node_n}, device_id_type=MESH).start()
        return carry

    lax.fori_loop(1, n, tell, 0)
    start_core(me, True)
    keep = pltpu.make_async_copy(block, every.at[me], local_sem)
    keep.start()
    meta[me] = place[me]

    def sides(t):
        return [(z >= t, z - t, True), (jnp.logical_and(t >= 1, z + t < outer), z + t, False)]

    slots = scaled.shape[1]
    tok, cols = held.shape[1:]

    def turn(i, carry):
        span = pl.ds(pl.multiple_of(i * part, part), part)
        turned[span, :] = down[:, span].T
        return carry

    def work(e):
        own = range(node_n)
        fetch = [pltpu.make_async_copy(every.at[e * node_n + c], held.at[c], held_sem.at[c]) for c in own]
        for one in fetch:
            one.start()
        spots = [meta[e * node_n + c] for c in own]
        names = lax.broadcasted_iota(jnp.int32, (slots, tok), 0).astype(f32)
        hits = [spot[0:1, :] == names for spot in spots]
        gains = [jnp.sum(jnp.where(hits[c], spots[c][1:2, :], 0.0), axis=1, keepdims=True) for c in own]
        picks = [hit.astype(f32).astype(bf16) for hit in hits]
        acc[...] = jnp.zeros_like(acc)
        for one in fetch:
            one.wait()

        def columns(i, carry):
            span = pl.ds(pl.multiple_of(i * part, part), part)
            got = [jnp.dot(picks[c], held[c, :, span], preferred_element_type=f32) for c in own]
            for c in own:
                scaled[e * node_n + c, :, span] = (got[c] * gains[c]).astype(bf16)
            acc[...] += jnp.dot(jnp.concatenate(got, axis=0).astype(bf16), turned[span, :],
                                preferred_element_type=f32)
            return carry

        lax.fori_loop(0, cols // part, columns, 0)
        for c in own:
            s = e * node_n + c
            u = acc[c * slots:(c + 1) * slots, :]
            partial[s] = (gains[c] * u).astype(bf16)
            slot = jnp.sum(u * hidden[s].astype(f32), axis=1, keepdims=True)
            back[s] = jnp.sum(jnp.where(hits[c], slot, 0.0), axis=0, keepdims=True)
            pltpu.make_async_copy(scaled.at[s], scaled_out.at[s], out_sem.at[0, s]).start()
            pltpu.make_async_copy(partial.at[s], partial_out.at[s], out_sem.at[1, s]).start()

    def told(j, carry):
        pltpu.make_async_remote_copy(
            src_ref=place.at[0], dst_ref=meta.at[0],
            send_sem=meta_send.at[j], recv_sem=meta_recv.at[j],
            device_id=dev(z, x, node), device_id_type=MESH).wait()
        return carry

    keep.wait()
    load_down.wait()
    load_hidden.wait()
    lax.fori_loop(0, cols // part, turn, 0)
    lax.fori_loop(1, n, told, 0)

    def step(t, carry):
        for exists, row, below in sides(t):
            s = source(row, x, node)

            @when(exists, t >= 1)
            def _():
                arrived(s)
                if below:
                    @pl.when(can_zu)
                    def _():
                        push(0, s, dev(z + 1, x, node))
                else:
                    @pl.when(can_zd)
                    def _():
                        push(1, s, dev(z - 1, x, node))
                start_x(s, can_xu, can_xd)
                start_core(s)

        for exists, row, _ in sides(t - 1):
            for far in range(1, inner):
                s_low = source(row, x - far, node)
                s_high = source(row, x + far, node)

                @when(exists, t >= 1, x >= far)
                def _():
                    arrived(s_low)
                    start_core(s_low)

                    @pl.when(can_xu)
                    def _():
                        push(2, s_low, dev(z, x + 1, node))

                @when(exists, t >= 1, x + far < inner)
                def _():
                    arrived(s_high)
                    start_core(s_high)

                    @pl.when(can_xd)
                    def _():
                        push(3, s_high, dev(z, x - 1, node))

        def each(e, carry):
            row, col = e // inner, e % inner
            away = jnp.abs(row - z) + jnp.where(col == x, 0, 1)

            @pl.when(away == t)
            def _():
                for k in range(1, node_n):
                    arrived(e * node_n + lax.rem(node + k, node_n))
                work(e)
            return carry

        lax.fori_loop(0, ep_n, each, 0)
        return carry

    lax.fori_loop(0, outer + 1, step, 0)

    def stored(s, carry):
        pltpu.make_async_copy(scaled.at[s], scaled_out.at[s], out_sem.at[0, s]).wait()
        pltpu.make_async_copy(partial.at[s], partial_out.at[s], out_sem.at[1, s]).wait()
        return carry

    lax.fori_loop(0, n, stored, 0)

    def ended(e, carry):
        s = e * node_n + node
        row, col = e // inner, e % inner
        mine = col == x

        @when(mine, row <= z, can_zu)
        def _():
            sent(0, s)

        @when(mine, row >= z, can_zd)
        def _():
            sent(1, s)

        @when(col <= x, can_xu)
        def _():
            sent(2, s)

        @when(col >= x, can_xd)
        def _():
            sent(3, s)

        for k in range(1, node_n):
            sent(3 + k, s)
        return carry

    lax.fori_loop(0, ep_n, ended, 0)


def gather(ep_n, inner, node_n, grad_out, place, down, hidden):
    n = ep_n * node_n
    tok, cols = grad_out.shape
    width = down.shape[0]
    slots = hidden.shape[1]
    part = 1792 if cols % 1792 == 0 else cols
    dma = pltpu.SemaphoreType.DMA
    return pl.pallas_call(
        functools.partial(gather_kernel, ep_n, inner, node_n, part),
        out_shape=(jax.ShapeDtypeStruct((n, tok, cols), bf16),
                   jax.ShapeDtypeStruct((n, slots, cols), bf16),
                   jax.ShapeDtypeStruct((n, slots, width), bf16),
                   jax.ShapeDtypeStruct((n, 1, tok), f32)),
        in_specs=[ANY, VM, ANY, ANY],
        out_specs=(ANY, ANY, ANY, VM),
        scratch_shapes=[
            pltpu.VMEM(place.shape, f32), pltpu.VMEM((width, cols), bf16),
            pltpu.VMEM((cols, width), bf16),
            pltpu.VMEM((n, slots, width), bf16), pltpu.VMEM((n, slots, cols), bf16),
            pltpu.VMEM((n, slots, width), bf16), pltpu.VMEM((node_n, tok, cols), bf16),
            pltpu.VMEM((node_n * slots, width), f32),
            dma, dma((2,)), dma((node_n,)), dma((2, n)),
            dma((3 + node_n, n)), dma((n,)), dma((n,)), dma((n,)),
        ],
        compiler_params=pltpu.CompilerParams(collective_id=0, has_side_effects=True,
                                             vmem_limit_bytes=56 << 20),
        name="gather",
    )(grad_out, place, down, hidden)


def weight_kernel(hidden, scaled, out, turned):
    @pl.when(pl.program_id(0) == 0)
    def _():
        turned[...] = hidden[...].T

    out[...] = jnp.dot(turned[...], scaled[...], preferred_element_type=f32).astype(bf16)


def weight(hidden, scaled):
    slots, width = hidden.shape
    cols = scaled.shape[1]
    part = 512 if cols % 512 == 0 else cols
    return pl.pallas_call(
        weight_kernel,
        grid=(cols // part,),
        out_shape=jax.ShapeDtypeStruct((width, cols), bf16),
        in_specs=[pl.BlockSpec((slots, width), lambda i: (0, 0)),
                  pl.BlockSpec((slots, part), lambda i: (0, i))],
        out_specs=pl.BlockSpec((width, part), lambda i: (0, i)),
        scratch_shapes=[pltpu.VMEM((width, slots), bf16)],
        compiler_params=pltpu.CompilerParams(vmem_limit_bytes=48 << 20),
        cost_estimate=pl.CostEstimate(flops=2 * slots * cols * width, transcendentals=0,
                                      bytes_accessed=2 * (slots * cols + slots * width + cols * width)),
        name="weight",
    )(hidden, scaled)


def gate_kernel(ep_n, node_n, dp_n, back, mask, chosen, whole, tokens, out, home, part, inbox,
                home_send, home_recv, send_a, recv_a, send_b, recv_b):
    ep, node, dp = lax.axis_index("ep"), lax.axis_index("node"), lax.axis_index("dp")
    n = ep_n * node_n
    me = ep * node_n + node
    everyone = n * dp_n

    def at(p, q):
        return {"ep": p // node_n, "node": p % node_n, "dp": q}

    def peer(j):
        return lax.rem(me + j % n, n), lax.rem(dp + j // n, dp_n)

    barrier = pltpu.get_barrier_semaphore()

    def greet(j, carry):
        p, q = peer(j)
        pl.semaphore_signal(barrier, inc=1, device_id=at(p, q), device_id_type=MESH)
        return carry

    lax.fori_loop(1, everyone, greet, 0)
    pl.semaphore_wait(barrier, everyone - 1)

    def home_copy(j):
        p, q = peer(j)
        return pltpu.make_async_remote_copy(
            src_ref=back.at[p], dst_ref=home.at[dp, me],
            send_sem=home_send.at[j], recv_sem=home_recv.at[j],
            device_id=at(p, q), device_id_type=MESH)

    def go_home(j, carry):
        home_copy(j).start()
        return carry

    lax.fori_loop(1, everyone, go_home, 0)
    home[dp, me] = back[me]

    def came_home(j, carry):
        home_copy(j).wait()
        return carry

    lax.fori_loop(1, everyone, came_home, 0)
    route = home[0, :, 0, :]
    for q in range(1, dp_n):
        route = route + home[q, :, 0, :]
    picked = chosen[...]
    all_of = whole[...]
    mixed = jnp.sum(route * picked, axis=0, keepdims=True) / all_of
    score_grad = route_scale / all_of * (route - mixed)
    logit = (mask[...] * score_grad * picked * (1.0 - picked)).astype(bf16)
    lanes = part.shape[2]
    for i in range(part.shape[1]):
        part[:, i, :] = jnp.dot(logit, tokens[:, i * lanes:(i + 1) * lanes], preferred_element_type=f32)

    def to_owner(j):
        p = lax.rem(me + j, n)
        return pltpu.make_async_remote_copy(
            src_ref=part.at[p], dst_ref=inbox.at[j],
            send_sem=send_a.at[j], recv_sem=recv_a.at[j],
            device_id=at(p, dp), device_id_type=MESH)

    def start_a(j, carry):
        to_owner(j).start()
        return carry

    def wait_a(j, carry):
        to_owner(j).wait()
        return carry

    lax.fori_loop(1, n, start_a, 0)
    lax.fori_loop(1, n, wait_a, 0)
    out[me] = lax.fori_loop(1, n, lambda j, acc: acc + inbox[j], part[me])

    def spread(j):
        p = lax.rem(me + j, n)
        return pltpu.make_async_remote_copy(
            src_ref=out.at[me], dst_ref=out.at[me],
            send_sem=send_b.at[j], recv_sem=recv_b.at[j],
            device_id=at(p, dp), device_id_type=MESH)

    def start_b(j, carry):
        spread(j).start()
        return carry

    def wait_b(j, carry):
        spread(j).wait()
        return carry

    lax.fori_loop(1, n, start_b, 0)
    lax.fori_loop(1, n, wait_b, 0)


def gate(ep_n, node_n, dp_n, back, mask, chosen, total, tokens):
    n = ep_n * node_n
    tok, cols = tokens.shape
    lanes = 128
    shape = (n, cols // lanes, lanes)
    dma = pltpu.SemaphoreType.DMA
    return pl.pallas_call(
        functools.partial(gate_kernel, ep_n, node_n, dp_n),
        out_shape=jax.ShapeDtypeStruct(shape, f32),
        in_specs=[VM] * 5,
        out_specs=VM,
        scratch_shapes=[pltpu.VMEM((dp_n, n, 1, tok), f32),
                        pltpu.VMEM(shape, f32), pltpu.VMEM(shape, f32),
                        dma((n * dp_n,)), dma((n * dp_n,)),
                        dma((n,)), dma((n,)), dma((n,)), dma((n,))],
        compiler_params=pltpu.CompilerParams(collective_id=1, has_side_effects=True,
                                             vmem_limit_bytes=24 << 20),
        cost_estimate=pl.CostEstimate(flops=2 * tok * cols * n, transcendentals=0,
                                      bytes_accessed=8 * n * cols),
        name="gate",
    )(back, mask, chosen, total, tokens).reshape(n, cols)


def body(ep_n, node_n, dp_n, grad_out, tokens, scores, expert_ids, hidden_act, down_weight):
    inner = 2 if ep_n <= 8 else 8
    mask, chosen, total, gains, rank = router(scores, expert_ids)
    place = jnp.stack([rank, gains.astype(f32)], axis=1)
    n = ep_n * node_n
    hidden = hidden_act[0]
    slots, width = hidden.shape
    most = slots // n
    fill = -most % 16
    apart = jnp.pad(hidden.reshape(n, most, width), ((0, 0), (0, fill), (0, 0)))
    every, scaled, partial, back = gather(ep_n, inner, node_n, grad_out, place, down_weight[0], apart)
    scaled = scaled[:, :most].reshape(slots, -1)
    partial = partial[:, :most].reshape(slots, width)
    hidden_grad = lax.psum_scatter(partial, "dp", scatter_dimension=0, tiled=True)[None]
    gate_grad = gate(ep_n, node_n, dp_n, back, mask, chosen, total, tokens)
    weight_grad = weight(hidden, scaled)[None]
    return (weight_grad, hidden_grad, gate_grad)


def solution(mesh):
    sizes = [mesh.shape[a] for a in ("ep", "node", "dp")]
    return jax.shard_map(
        functools.partial(body, *sizes),
        mesh=mesh,
        in_specs=(
            P(AX, "dp"),
            P(AX, "dp"),
            P(AX, None),
            P(AX, None),
            P(AX, None, None),
            P(AX, None, "dp"),
        ),
        out_specs=(P(AX, None, "dp"), P(AX, "dp", None), P(None, "dp")),
        check_vma=False,
    )
```
